32 devices in a mesh: section: 4 (over y, x), patch: 2 (over core), chan: 4 (over z).
Axes of the slice: x: 2, y: 2, z: 4, core: 2. Of those that a mesh axis runs over, the one named last changes fastest.
Arguments:
- cond: bfloat16 [4, 128, 16, 128], P('section', 'chan', 'patch'), may hold values from -20 to 20
- noise: bfloat16 [4, 128, 16, 128], P('section', 'chan', 'patch'), may hold values from -6 to 6
- conv_weight: bfloat16 [4, 9, 128, 128], P('section', None, 'chan'), may hold values from -0.1875 to 0.1875
- mix_weight: bfloat16 [4, 128, 128], P('section', 'chan'), may hold values from -0.5 to 0.5
- norm_gain: float32 [4, 128], P('section', 'chan'), may hold values from 0.1 to 1.9
- norm_bias: float32 [4, 128], P('section', 'chan'), may hold values from -3 to 3
Outputs:
- field: bfloat16 [4, 128, 16, 128], P('section', 'chan', 'patch')
The draws below stay inside these ranges and needn't reach their ends.
All inputs are finite; a program needn't handle non-finite values.
Results may differ from the reference program's by a relative error of at most 0.012.
Values may be sent and summed in bfloat16 or wider, within the bound.
A program may use at most 64 MiB of HBM per device.

```python
import jax
import jax.numpy as jnp
from jax import lax

C = 128
GROUPS = 32
COLS = 128
LAYERS = 4
MB = 4
H = 16


def draw_cond(key, part):
    key = jax.random.fold_in(key, 7)
    first_key, second_key = jax.random.split(key)
    row_axis = jnp.arange(H, dtype=jnp.float32)
    row_scale = jnp.exp(jnp.log(10.0) * row_axis / max(H - 1, 1)) / 10.0
    base = jnp.clip(jax.random.normal(first_key, (MB, C, H, COLS), jnp.float32), -5.0, 5.0)
    chan_scale = jnp.exp(jax.random.uniform(second_key, (C,), jnp.float32, 0.0, jnp.log(3.0)))
    return (base * chan_scale[None, :, None, None] * row_scale[None, None, :, None]).astype(jnp.bfloat16)


def steps_of(own_key, dims, cuts, least, top_value):
    def one(position, shards_of):
        draws = jax.random.uniform(jax.random.fold_in(jax.random.fold_in(own_key, 6), position), (shards_of,), jnp.float32, least / len(cuts), top_value / len(cuts))
        return jnp.repeat(jnp.exp(draws), dims[position] // shards_of).reshape((-1,) + (1,) * (len(dims) - position - 1))

    loudness = one(*cuts[0])
    for cut in cuts[1:]:
        loudness = loudness * one(*cut)
    return loudness


def bell_draw(stream_key, dims, deviation, most, cuts=(), kind=jnp.bfloat16):
    result = deviation * jax.random.normal(stream_key, dims, jnp.float32)
    if cuts:
        result = result * steps_of(stream_key, dims, cuts, -0.22, 0.18)
    return jnp.clip(result, -most, most).astype(kind)


def setup_inputs(seed: int = 0) -> dict:
    key_of = jax.random.split(jax.random.key(seed), 7)
    cond = draw_cond(jax.random.fold_in(key_of[6], 71), 0)
    noise = bell_draw(key_of[1], (MB, C, H, COLS), 1.0, 6.0, ((0, 4), (1, 4), (2, 2)))
    conv_weight = bell_draw(key_of[2], (LAYERS, 9, C, C), (9 * C) ** -0.5, 0.1875, ((0, 4), (2, 4)))
    mix_weight = bell_draw(key_of[3], (LAYERS, C, C), C ** -0.5, 0.5, ((0, 4), (1, 4)))
    norm_gain = jnp.clip(1.0 + 0.18 * jax.random.normal(key_of[4], (LAYERS, C), jnp.float32), 0.1, 1.9)
    norm_bias = bell_draw(key_of[5], (LAYERS, C), 0.5, 3.0, ((0, 4), (1, 4)), jnp.float32)
    return dict(cond=cond, noise=noise, conv_weight=conv_weight, mix_weight=mix_weight, norm_gain=norm_gain, norm_bias=norm_bias)


def run_block(inputs, tap_weight, mix_matrix, gain_row, bias_row):
    padded = jnp.pad(inputs, ((0, 0), (1, 1), (1, 1))).astype(jnp.float32)
    conv_total = jnp.zeros((C, H, COLS), jnp.float32)
    for tap_index in range(9):
        row_off, col_off = divmod(tap_index, 3)
        window = padded[:, row_off:row_off + H, col_off:col_off + COLS]
        conv_total = conv_total + jnp.einsum('oc,chw->ohw', tap_weight[tap_index].astype(jnp.float32), window)
    grouped = conv_total.reshape(GROUPS, C // GROUPS, H, COLS)
    group_mean = lax.optimization_barrier(jnp.mean(grouped, axis=(1, 2, 3), keepdims=True))
    group_square = lax.optimization_barrier(jnp.mean(grouped * grouped, axis=(1, 2, 3), keepdims=True))
    variance = group_square - group_mean * group_mean
    normed = ((grouped - group_mean) / jnp.sqrt(variance + 1e-05)).reshape(C, H, COLS)
    normed = normed * gain_row[:, None, None] + bias_row[:, None, None]
    acted = jax.nn.silu(normed).astype(jnp.bfloat16)
    return jnp.einsum('oc,chw->ohw', mix_matrix.astype(jnp.float32), acted.astype(jnp.float32))

def reference(cond, noise, conv_weight, mix_weight, norm_gain, norm_bias):

    def one_sample(pair):
        cond_one, noise_one = pair
        first_out = run_block(cond_one, conv_weight[0], mix_weight[0], norm_gain[0], norm_bias[0])
        mean_field = (cond_one.astype(jnp.float32) + first_out).astype(jnp.bfloat16)
        sample = noise_one
        for layer_index in range(1, LAYERS):
            inputs = (sample.astype(jnp.float32) + mean_field.astype(jnp.float32)).astype(jnp.bfloat16)
            denoised = run_block(inputs, conv_weight[layer_index], mix_weight[layer_index], norm_gain[layer_index], norm_bias[layer_index])
            before = sample.astype(jnp.float32)
            sample = (before + 0.5 * (denoised - before)).astype(jnp.bfloat16)
        return (sample.astype(jnp.float32) + mean_field.astype(jnp.float32)).astype(jnp.bfloat16)
    return lax.map(one_sample, (cond, noise))
```

```python
import functools

import jax
import jax.numpy as jnp
from jax import lax
from jax.experimental import pallas as pl
from jax.experimental.pallas import tpu as pltpu
from jax.sharding import PartitionSpec as P

C = 128
GROUPS = 32


def with_halo(cells, sides, width):
    for axis, dim in sides:
        count = lax.axis_size(axis)
        ends = count - 1
        head = lax.slice_in_dim(cells, 0, width, axis=dim)
        tail = lax.slice_in_dim(cells, cells.shape[dim] - width, cells.shape[dim], axis=dim)
        cells = jnp.concatenate(
            [
                lax.ppermute(tail, axis, [(i, (i + 1) % count) for i in range(ends)]),
                cells,
                lax.ppermute(head, axis, [((i + 1) % count, i) for i in range(ends)]),
            ],
            axis=dim,
        )
    return cells


def from_root(value, axis, source):
    kept = jnp.where(lax.axis_index(axis) == source, value, 0).astype(value.dtype)
    return lax.psum(kept, axis)


def conv_taps(running, row_padded, tap_weight, num_rows, num_cols):
    padded = jnp.pad(row_padded, ((0, 0), (0, 0), (0, 0), (1, 1)))
    for tap_index in range(9):
        row_off, col_off = divmod(tap_index, 3)
        window = padded[:, :, row_off : row_off + num_rows, col_off : col_off + num_cols]
        running = running + jnp.einsum(
            "oc,bchw->bohw", tap_weight[tap_index], window, preferred_element_type=jnp.float32
        )
    return running


def group_norm(conv_total, gain_row, bias_row):
    batch_size, out_chans, num_rows, num_cols = conv_total.shape
    group_size = C // GROUPS
    grouped = conv_total.reshape(
        batch_size, out_chans // group_size, group_size, num_rows, num_cols
    )
    local_sums = jnp.sum(grouped, axis=(2, 3, 4))
    local_squares = jnp.sum(grouped * grouped, axis=(2, 3, 4))
    sums, squares = lax.psum((local_sums, local_squares), "patch")
    entries = group_size * num_rows * num_cols * lax.axis_size("patch")
    group_mean = sums / entries
    variance = squares / entries - group_mean * group_mean
    scale_now = 1.0 / jnp.sqrt(variance + 1e-05)
    normed = (grouped - group_mean[:, :, None, None, None]) * scale_now[:, :, None, None, None]
    normed = normed.reshape(batch_size, out_chans, num_rows, num_cols)
    normed = normed * gain_row[None, :, None, None] + bias_row[None, :, None, None]
    return jax.nn.silu(normed).astype(jnp.bfloat16)


def apply_block(inputs, params):
    tap_weight, mix_matrix, gain_row, bias_row = params
    batch_size = inputs.shape[0]
    num_rows = inputs.shape[2]
    num_cols = inputs.shape[3]
    out_chans = tap_weight.shape[1]
    padded = with_halo(inputs, (("patch", 2),), 1)
    empty = jnp.zeros((batch_size, out_chans, num_rows, num_cols), jnp.float32)
    weight_part = tap_weight
    conv_total = conv_taps(
        empty, lax.all_gather(padded, "chan", axis=1, tiled=True), weight_part, num_rows, num_cols
    )
    acted = group_norm(conv_total, gain_row, bias_row)
    weight_part = mix_matrix
    return jnp.einsum(
        "oc,bchw->bohw",
        weight_part,
        lax.all_gather(acted, "chan", axis=1, tiled=True),
        preferred_element_type=jnp.float32,
    )


def prepare(params):
    tap_weight = params[0][0]
    mix_matrix = params[1][0]
    gain_row = params[2][0]
    bias_row = params[3][0]
    return (tap_weight, mix_matrix, gain_row, bias_row)


def body(cond, noise, conv_weight, mix_weight, norm_gain, norm_bias):
    sections = lax.axis_size("section")
    mean_field = cond
    sample = noise
    for layer_index in range(sections):
        shared = (
            from_root(conv_weight, "section", layer_index),
            from_root(mix_weight, "section", layer_index),
            from_root(norm_gain.astype(jnp.bfloat16), "section", layer_index).astype(
                norm_gain.dtype
            ),
            from_root(norm_bias.astype(jnp.bfloat16), "section", layer_index).astype(
                norm_bias.dtype
            ),
        )
        params = prepare(shared)
        if layer_index == 0:
            first_out = apply_block(cond, params)
            mean_field = (cond.astype(jnp.float32) + first_out).astype(jnp.bfloat16)
        else:
            inputs = (sample.astype(jnp.float32) + mean_field.astype(jnp.float32)).astype(
                jnp.bfloat16
            )
            denoised = apply_block(inputs, params)
            before = sample.astype(jnp.float32)
            sample = (before + 0.5 * (denoised - before)).astype(jnp.bfloat16)
    result = (sample.astype(jnp.float32) + mean_field.astype(jnp.float32)).astype(jnp.bfloat16)
    return result


MESH = pl.DeviceIdType.MESH
AXES = ("section", "patch", "chan")


def remote(src, dst, send_sem, recv_sem, section, patch, chan):
    return pltpu.make_async_remote_copy(
        src_ref=src,
        dst_ref=dst,
        send_sem=send_sem,
        recv_sem=recv_sem,
        device_id=(section, patch, chan),
        device_id_type=MESH,
    )


def whole_kernel(
    sections, chans, rows, cols,
    cond_in, noise_in, conv_in, mix_in, gb_in, out_ref,
    cond_f, noise_f, mean_f, weights, gb, shifted, conv_f,
    load_sem, wz_send, wz_recv, ws_send, ws_recv, wc_send, wc_recv,
    gz_send, gz_recv, gs_send, gs_recv,
    cz_send, cz_recv, cc_send, cc_recv, nz_send, nz_recv, nc_send, nc_recv,
):
    s = lax.axis_index("section")
    p = lax.axis_index("patch")
    z = lax.axis_index("chan")
    other = 1 - p
    taps = 10
    half = taps // 2
    part = C // chans
    cells = rows * cols
    sec_peers = [lax.rem(s + d, sections) for d in range(1, sections)]
    z_peers = [lax.rem(z + d, chans) for d in range(1, chans)]

    def band(index):
        return pl.ds(pl.multiple_of(index * part, part), part)

    mine = band(z)
    loads = [
        pltpu.make_async_copy(
            conv_in.at[pl.ds(p * half, half - 1)],
            weights.at[s, pl.ds(p * half, half - 1), mine, :],
            load_sem.at[0],
        ),
        pltpu.make_async_copy(gb_in, gb.at[s, z], load_sem.at[2]),
        pltpu.make_async_copy(cond_in, cond_f.at[p, mine, :], load_sem.at[3]),
        pltpu.make_async_copy(noise_in, noise_f.at[p, mine, :], load_sem.at[4]),
    ]
    for copy in loads:
        copy.start()
    fifth = weights.at[s, p * half + half - 1, mine, :]

    @pl.when(p == 0)
    def _():
        pltpu.make_async_copy(conv_in.at[half - 1], fifth, load_sem.at[1]).start()

    @pl.when(p != 0)
    def _():
        pltpu.make_async_copy(mix_in, fifth, load_sem.at[1]).start()

    barrier = pltpu.get_barrier_semaphore()
    for peer in sec_peers:
        pl.semaphore_signal(barrier, inc=1, device_id=(peer, p, z), device_id_type=MESH)
    for peer in z_peers:
        pl.semaphore_signal(barrier, inc=1, device_id=(s, p, peer), device_id_type=MESH)
    pl.semaphore_signal(barrier, inc=1, device_id=(s, other, z), device_id_type=MESH)
    pl.semaphore_wait(barrier, sections + chans - 1)

    def w_half(layer, which):
        return weights.at[layer, pl.ds(which * half, half)]

    def w_shard(owner):
        return weights.at[s, pl.ds(p * half, half), band(owner), :]

    def w_z(d, owner):
        return remote(w_shard(owner), w_shard(owner), wz_send.at[d], wz_recv.at[owner], s, p, z_peers[d])

    def g_z(d, owner):
        return remote(gb.at[s, owner], gb.at[s, owner], gz_send.at[d], gz_recv.at[owner], s, p, z_peers[d])

    def w_s(d, layer):
        return remote(w_half(layer, p), w_half(layer, p), ws_send.at[d], ws_recv.at[layer], sec_peers[d], p, z)

    def g_s(d, layer):
        return remote(gb.at[layer], gb.at[layer], gs_send.at[d], gs_recv.at[layer], sec_peers[d], p, z)

    def w_c(layer, which):
        return remote(w_half(layer, which), w_half(layer, which), wc_send.at[layer], wc_recv.at[layer], s, other, z)

    def f_z(field, send, recv, d, owner):
        block = field.at[p, band(owner), :]
        return remote(block, block, send.at[d], recv.at[owner], s, p, z_peers[d])

    def f_c(field, send, recv, which, owner):
        block = field.at[which, band(owner), :]
        return remote(block, block, send.at[owner], recv.at[owner], s, other, z)

    steps = range(chans - 1)
    for copy in loads[:2]:
        copy.wait()
    pltpu.make_async_copy(mix_in, fifth, load_sem.at[1]).wait()
    for d in steps:
        w_z(d, z).start()
        g_z(d, z).start()
    loads[2].wait()
    for d in steps:
        f_z(cond_f, cz_send, cz_recv, d, z).start()
    f_c(cond_f, cc_send, cc_recv, p, z).start()
    loads[3].wait()

    zero_row = jnp.zeros((3 * C, cols), jnp.bfloat16)
    shifted[:, 0:cols] = zero_row
    shifted[:, (rows + 1) * cols : (rows + 2) * cols] = zero_row

    for d in steps:
        w_z(d, z_peers[d]).wait_recv()
        g_z(d, z_peers[d]).wait_recv()
    for d in range(sections - 1):
        w_s(d, s).start()
        g_s(d, s).start()
    w_c(s, p).start()
    for d in steps:
        f_z(noise_f, nz_send, nz_recv, d, z).start()
    f_c(noise_f, nc_send, nc_recv, p, z).start()

    def forward_field(field, z_send, z_recv, c_send, c_recv):
        for d in steps:
            f_z(field, z_send, z_recv, d, z_peers[d]).wait_recv()
            f_c(field, c_send, c_recv, p, z_peers[d]).start()
        for owner in range(chans):
            f_c(field, c_send, c_recv, other, owner).wait_recv()

    def forward_layer(layer):
        @pl.when(s != layer)
        def _():
            w_s(0, layer).wait_recv()
            g_s(0, layer).wait_recv()
            w_c(layer, p).start()

    lane = lax.broadcasted_iota(jnp.int32, (C, cols), 1)
    chan_row = lax.broadcasted_iota(jnp.int32, (C, cols), 0)
    per_patch = rows // 2

    def put_row(values, row):
        base = (row + 1) * cols
        left = jnp.where(lane == 0, 0.0, pltpu.roll(values, 1, 1))
        right = jnp.where(lane == cols - 1, 0.0, pltpu.roll(values, cols - 1, 1))
        shifted[0:C, pl.ds(base, cols)] = left.astype(jnp.bfloat16)
        shifted[C : 2 * C, pl.ds(base, cols)] = values.astype(jnp.bfloat16)
        shifted[2 * C : 3 * C, pl.ds(base, cols)] = right.astype(jnp.bfloat16)

    def group_sum(values):
        total = jnp.broadcast_to(jnp.sum(values, axis=1, keepdims=True), (C, cols))
        for bit in (1, 2):
            pair = jnp.where(
                (chan_row // bit) % 2 == 0, pltpu.roll(total, C - bit, 0), pltpu.roll(total, bit, 0)
            )
            total = total + pair
        return total

    chunk_rows = 4
    chunk = chunk_rows * cols
    per_half = per_patch // chunk_rows

    def conv_and_stats(layer):
        lhs = jnp.concatenate([weights[layer, tap] for tap in range(9)], axis=1)
        sums = jnp.zeros((C, cols), jnp.float32)
        squares = jnp.zeros((C, cols), jnp.float32)
        for q in range(rows // chunk_rows):
            rhs = jnp.concatenate(
                [shifted[:, q * chunk + a * cols : q * chunk + a * cols + chunk] for a in range(3)],
                axis=0,
            )
            got = jnp.dot(lhs, rhs, preferred_element_type=jnp.float32)
            conv_f[q // per_half, :, (q % per_half) * chunk : (q % per_half + 1) * chunk] = got
            for r in range(chunk_rows):
                tile = got[:, r * cols : (r + 1) * cols]
                sums = sums + tile
                squares = squares + tile * tile
        turned = jnp.concatenate(
            [gb[layer, owner] for owner in range(chans)]
            + [jnp.zeros((C - 8 * chans, cols), jnp.float32)],
            axis=0,
        ).T
        gain = jnp.concatenate(
            [turned[0:part, 8 * owner : 8 * owner + 1] for owner in range(chans)], axis=0
        )
        bias = jnp.concatenate(
            [turned[0:part, 8 * owner + 1 : 8 * owner + 2] for owner in range(chans)], axis=0
        )
        entries = (C // GROUPS) * cells
        mu = group_sum(sums) / entries
        var = group_sum(squares) / entries - mu * mu
        scale = 0.5 * gain / jnp.sqrt(var + 1e-05)
        return scale, 0.5 * bias - mu * scale

    def acted_of(conv, scale, shift):
        tiles = []
        for r in range(chunk_rows):
            h = conv[:, r * cols : (r + 1) * cols] * scale + shift
            tiles.append((h + h * jnp.tanh(h)).astype(jnp.bfloat16))
        return jnp.concatenate(tiles, axis=1)

    forward_field(cond_f, cz_send, cz_recv, cc_send, cc_recv)
    for row in range(rows):
        at = (row % per_patch) * cols
        put_row(cond_f[row // per_patch, :, at : at + cols].astype(jnp.float32), row)
    forward_layer(0)
    w_c(0, other).wait_recv()

    for layer in range(sections):
        last = layer == sections - 1
        scale, shift = conv_and_stats(layer)
        if layer == 0:
            for later in range(1, sections):
                forward_layer(later)
            forward_field(noise_f, nz_send, nz_recv, nc_send, nc_recv)
            for d in steps:
                f_z(noise_f, nz_send, nz_recv, d, z).wait_send()
            for owner in range(chans):
                f_c(noise_f, nc_send, nc_recv, p, owner).wait_send()
        if not last:
            for q in range(rows // chunk_rows):
                where = q // per_half
                span = slice((q % per_half) * chunk, (q % per_half + 1) * chunk)
                acted = acted_of(conv_f[where, :, span], scale, shift)
                out = jnp.dot(weights[layer, 9], acted, preferred_element_type=jnp.float32)
                before = noise_f[where, :, span].astype(jnp.float32)
                if layer == 0:
                    mean = (cond_f[where, :, span].astype(jnp.float32) + out).astype(jnp.bfloat16)
                    mean_f[where, :, span] = mean
                    sample = before
                else:
                    mean = mean_f[where, :, span]
                    sample = (before + 0.5 * (out - before)).astype(jnp.bfloat16)
                    noise_f[where, :, span] = sample
                    sample = sample.astype(jnp.float32)
                inputs = (sample + mean.astype(jnp.float32)).astype(jnp.bfloat16).astype(jnp.float32)
                for r in range(chunk_rows):
                    put_row(inputs[:, r * cols : (r + 1) * cols], q * chunk_rows + r)
            w_c(layer + 1, other).wait_recv()
        else:
            for q in range(per_half):
                span = slice(q * chunk, (q + 1) * chunk)
                acted = acted_of(conv_f[p, :, span], scale, shift)
                out = jnp.dot(weights[layer, 9, mine, :], acted, preferred_element_type=jnp.float32)
                before = noise_f[p, mine, span].astype(jnp.float32)
                sample = (before + 0.5 * (out - before)).astype(jnp.bfloat16).astype(jnp.float32)
                out_ref[:, span] = (sample + mean_f[p, mine, span].astype(jnp.float32)).astype(
                    jnp.bfloat16
                )

    for d in steps:
        w_z(d, z).wait_send()
        g_z(d, z).wait_send()
        f_z(cond_f, cz_send, cz_recv, d, z).wait_send()
    for d in range(sections - 1):
        w_s(d, s).wait_send()
        g_s(d, s).wait_send()
    for layer in range(sections):
        w_c(layer, p).wait_send()
    for owner in range(chans):
        f_c(cond_f, cc_send, cc_recv, p, owner).wait_send()


def fused_body(cond, noise, conv_weight, mix_weight, norm_gain, norm_bias):
    sections = lax.axis_size("section")
    chans = lax.axis_size("chan")
    _, part, own_rows, cols = cond.shape
    rows = 2 * own_rows
    own = own_rows * cols
    gb = jnp.pad(
        jnp.concatenate([norm_gain, norm_bias], axis=0), ((0, 6), (0, 128 - part))
    )
    dma = pltpu.SemaphoreType.DMA
    near, far = chans - 1, chans
    out = pl.pallas_call(
        functools.partial(whole_kernel, sections, chans, rows, cols),
        out_shape=jax.ShapeDtypeStruct((part, own), jnp.bfloat16),
        in_specs=[pl.BlockSpec(memory_space=pl.ANY)] * 5,
        out_specs=pl.BlockSpec(memory_space=pltpu.VMEM),
        scratch_shapes=[
            pltpu.VMEM((2, C, own), jnp.bfloat16),
            pltpu.VMEM((2, C, own), jnp.bfloat16),
            pltpu.VMEM((2, C, own), jnp.bfloat16),
            pltpu.VMEM((sections, 10, C, C), jnp.bfloat16),
            pltpu.VMEM((sections, chans, 8, 128), jnp.float32),
            pltpu.VMEM((3 * C, (rows + 2) * cols), jnp.bfloat16),
            pltpu.VMEM((2, C, own), jnp.float32),
            dma((5,)),
            dma((near,)), dma((far,)), dma((sections - 1,)), dma((sections,)),
            dma((sections,)), dma((sections,)),
            dma((near,)), dma((far,)), dma((sections - 1,)), dma((sections,)),
            dma((near,)), dma((far,)), dma((far,)), dma((far,)),
            dma((near,)), dma((far,)), dma((far,)), dma((far,)),
        ],
        compiler_params=pltpu.CompilerParams(
            collective_id=0, has_side_effects=True, vmem_limit_bytes=40 * 1024 * 1024
        ),
    )(
        cond.reshape(part, own), noise.reshape(part, own), conv_weight[0], mix_weight[0], gb
    )
    return out.reshape(1, part, own_rows, cols)


def solution(mesh):
    whole = mesh.shape["patch"] == 2
    return jax.shard_map(
        fused_body if whole else body,
        mesh=mesh,
        in_specs=(
            P("section", "chan", "patch", None),
            P("section", "chan", "patch", None),
            P("section", None, "chan", None),
            P("section", "chan", None),
            P("section", "chan"),
            P("section", "chan"),
        ),
        out_specs=P("section", "chan", "patch", None),
        check_vma=False,
    )
```

```python
import functools

import jax
import jax.numpy as jnp
from jax import lax
from jax.experimental import pallas as pl
from jax.experimental.pallas import tpu as pltpu
from jax.sharding import PartitionSpec as P

C = 128
GROUPS = 32


def with_halo(cells, sides, width):
    for axis, dim in sides:
        count = lax.axis_size(axis)
        ends = count - 1
        head = lax.slice_in_dim(cells, 0, width, axis=dim)
        tail = lax.slice_in_dim(cells, cells.shape[dim] - width, cells.shape[dim], axis=dim)
        cells = jnp.concatenate(
            [
                lax.ppermute(tail, axis, [(i, (i + 1) % count) for i in range(ends)]),
                cells,
                lax.ppermute(head, axis, [((i + 1) % count, i) for i in range(ends)]),
            ],
            axis=dim,
        )
    return cells


def from_root(value, axis, source):
    kept = jnp.where(lax.axis_index(axis) == source, value, 0).astype(value.dtype)
    return lax.psum(kept, axis)


def conv_taps(running, row_padded, tap_weight, num_rows, num_cols):
    padded = jnp.pad(row_padded, ((0, 0), (0, 0), (0, 0), (1, 1)))
    for tap_index in range(9):
        row_off, col_off = divmod(tap_index, 3)
        window = padded[:, :, row_off : row_off + num_rows, col_off : col_off + num_cols]
        running = running + jnp.einsum(
            "oc,bchw->bohw", tap_weight[tap_index], window, preferred_element_type=jnp.float32
        )
    return running


def group_norm(conv_total, gain_row, bias_row):
    batch_size, out_chans, num_rows, num_cols = conv_total.shape
    group_size = C // GROUPS
    grouped = conv_total.reshape(
        batch_size, out_chans // group_size, group_size, num_rows, num_cols
    )
    local_sums = jnp.sum(grouped, axis=(2, 3, 4))
    local_squares = jnp.sum(grouped * grouped, axis=(2, 3, 4))
    sums, squares = lax.psum((local_sums, local_squares), "patch")
    entries = group_size * num_rows * num_cols * lax.axis_size("patch")
    group_mean = sums / entries
    variance = squares / entries - group_mean * group_mean
    scale_now = 1.0 / jnp.sqrt(variance + 1e-05)
    normed = (grouped - group_mean[:, :, None, None, None]) * scale_now[:, :, None, None, None]
    normed = normed.reshape(batch_size, out_chans, num_rows, num_cols)
    normed = normed * gain_row[None, :, None, None] + bias_row[None, :, None, None]
    return jax.nn.silu(normed).astype(jnp.bfloat16)


def apply_block(inputs, params):
    tap_weight, mix_matrix, gain_row, bias_row = params
    batch_size = inputs.shape[0]
    num_rows = inputs.shape[2]
    num_cols = inputs.shape[3]
    out_chans = tap_weight.shape[1]
    padded = with_halo(inputs, (("patch", 2),), 1)
    empty = jnp.zeros((batch_size, out_chans, num_rows, num_cols), jnp.float32)
    weight_part = tap_weight
    conv_total = conv_taps(
        empty, lax.all_gather(padded, "chan", axis=1, tiled=True), weight_part, num_rows, num_cols
    )
    acted = group_norm(conv_total, gain_row, bias_row)
    weight_part = mix_matrix
    return jnp.einsum(
        "oc,bchw->bohw",
        weight_part,
        lax.all_gather(acted, "chan", axis=1, tiled=True),
        preferred_element_type=jnp.float32,
    )


def prepare(params):
    tap_weight = params[0][0]
    mix_matrix = params[1][0]
    gain_row = params[2][0]
    bias_row = params[3][0]
    return (tap_weight, mix_matrix, gain_row, bias_row)


def body(cond, noise, conv_weight, mix_weight, norm_gain, norm_bias):
    sections = lax.axis_size("section")
    mean_field = cond
    sample = noise
    for layer_index in range(sections):
        shared = (
            from_root(conv_weight, "section", layer_index),
            from_root(mix_weight, "section", layer_index),
            from_root(norm_gain.astype(jnp.bfloat16), "section", layer_index).astype(
                norm_gain.dtype
            ),
            from_root(norm_bias.astype(jnp.bfloat16), "section", layer_index).astype(
                norm_bias.dtype
            ),
        )
        params = prepare(shared)
        if layer_index == 0:
            first_out = apply_block(cond, params)
            mean_field = (cond.astype(jnp.float32) + first_out).astype(jnp.bfloat16)
        else:
            inputs = (sample.astype(jnp.float32) + mean_field.astype(jnp.float32)).astype(
                jnp.bfloat16
            )
            denoised = apply_block(inputs, params)
            before = sample.astype(jnp.float32)
            sample = (before + 0.5 * (denoised - before)).astype(jnp.bfloat16)
    result = (sample.astype(jnp.float32) + mean_field.astype(jnp.float32)).astype(jnp.bfloat16)
    return result


MESH = pl.DeviceIdType.MESH
AXES = ("section", "patch", "chan")


def remote(src, dst, send_sem, recv_sem, section, patch, chan):
    return pltpu.make_async_remote_copy(
        src_ref=src,
        dst_ref=dst,
        send_sem=send_sem,
        recv_sem=recv_sem,
        device_id=(section, patch, chan),
        device_id_type=MESH,
    )


def whole_kernel(
    sections, chans, rows, cols,
    cond_in, noise_in, conv_in, mix_in, gb_in, out_ref,
    cond_f, noise_f, mean_f, weights, shifted, conv_f,
    load_sem, wz_send, wz_recv, ws_send, ws_recv, wc_send, wc_recv,
    cz_send, cz_recv, cc_send, cc_recv, nz_send, nz_recv, nc_send, nc_recv,
):
    s = lax.axis_index("section")
    p = lax.axis_index("patch")
    z = lax.axis_index("chan")
    other = 1 - p
    taps = 12
    half = taps // 2
    part = C // chans
    cells = rows * cols
    sec_peers = [lax.rem(s + d, sections) for d in range(1, sections)]
    z_peers = [lax.rem(z + d, chans) for d in range(1, chans)]

    def band(index):
        return pl.ds(pl.multiple_of(index * part, part), part)

    mine = band(z)
    cond_load = pltpu.make_async_copy(cond_in, cond_f.at[p, mine, :], load_sem.at[0])
    noise_load = pltpu.make_async_copy(noise_in, noise_f.at[p, mine, :], load_sem.at[1])
    mix_load = pltpu.make_async_copy(mix_in, weights.at[s, 9, mine, :], load_sem.at[2])

    def conv_load(first, count):
        return pltpu.make_async_copy(
            conv_in.at[pl.ds(first, count)],
            weights.at[s, pl.ds(first, count), mine, :],
            load_sem.at[3],
        )

    cond_load.start()

    @pl.when(p == 0)
    def _():
        conv_load(0, half).start()

    @pl.when(p != 0)
    def _():
        conv_load(half, 9 - half).start()
        mix_load.start()

    noise_load.start()

    barrier = pltpu.get_barrier_semaphore()
    for peer in sec_peers:
        pl.semaphore_signal(barrier, inc=1, device_id=(peer, p, z), device_id_type=MESH)
    for peer in z_peers:
        pl.semaphore_signal(barrier, inc=1, device_id=(s, p, peer), device_id_type=MESH)
    pl.semaphore_signal(barrier, inc=1, device_id=(s, other, z), device_id_type=MESH)
    pl.semaphore_wait(barrier, sections + chans - 1)

    @pl.when(p == 0)
    def _():
        conv_load(0, half).wait()

    @pl.when(p != 0)
    def _():
        exact = gb_in[...]
        high = exact.astype(jnp.bfloat16)
        rest = exact - high.astype(jnp.float32)
        middle = rest.astype(jnp.bfloat16)
        low = (rest - middle.astype(jnp.float32)).astype(jnp.bfloat16)
        column = lax.broadcasted_iota(jnp.int32, exact.shape, 1)
        pieces = jnp.where(
            column < 2,
            high.astype(jnp.float32),
            jnp.where(column < 4, middle.astype(jnp.float32), low.astype(jnp.float32)),
        )
        weights[s, 10, mine, :] = pieces.astype(jnp.bfloat16)
        weights[s, 11, mine, :] = jnp.zeros_like(high)
        conv_load(half, 9 - half).wait()
        mix_load.wait()

    def w_half(layer, which):
        return weights.at[layer, pl.ds(which * half, half)]

    def w_shard(layer, owner):
        return weights.at[layer, pl.ds(p * half, half), band(owner), :]

    def w_z(way, k, owner):
        block = w_shard(s, owner)
        return remote(block, block, wz_send.at[way, k], wz_recv.at[owner], s, p, z + 1 - 2 * way)

    def w_s(d, layer, owner):
        block = w_shard(layer, owner)
        return remote(block, block, ws_send.at[d, owner], ws_recv.at[layer, owner], sec_peers[d], p, z)

    def w_c(layer, which):
        return remote(w_half(layer, which), w_half(layer, which), wc_send.at[layer], wc_recv.at[layer], s, other, z)

    def f_z(field, send, recv, way, k, owner):
        block = field.at[p, band(owner), :]
        return remote(block, block, send.at[way, k], recv.at[owner], s, p, z + 1 - 2 * way)

    def f_c(field, send, recv, which, owner):
        block = field.at[which, band(owner), :]
        return remote(block, block, send.at[owner], recv.at[owner], s, other, z)

    cond_z = functools.partial(f_z, cond_f, cz_send, cz_recv)
    cond_c = functools.partial(f_c, cond_f, cc_send, cc_recv)
    noise_z = functools.partial(f_z, noise_f, nz_send, nz_recv)
    noise_c = functools.partial(f_c, noise_f, nc_send, nc_recv)

    def to_sections(owner):
        for d in range(sections - 1):
            w_s(d, s, owner).start()

    def along(way, k):
        owner = z - k if way == 0 else z + k
        here = z >= k if way == 0 else z + k < chans
        going = z < chans - 1 if way == 0 else z > 0
        return owner, here, here & going

    def hop(copy, aside, k):
        if k == 0:
            for way in range(2):
                owner, _, sends = along(way, 0)

                @pl.when(sends)
                def _():
                    copy(way, 0, owner).start()

            aside(z)
            return
        for way in range(2):
            owner, here, sends = along(way, k)

            @pl.when(here)
            def _():
                copy(way, 0, owner).wait_recv()
                if k < chans - 1:

                    @pl.when(sends)
                    def _():
                        copy(way, k, owner).start()

                aside(owner)

    def sent(copy):
        for way in range(2):
            for k in range(chans - 1):
                owner, _, sends = along(way, k)

                @pl.when(sends)
                def _():
                    copy(way, k, owner).wait_send()

    def cond_aside(owner):
        cond_c(p, owner).start()

    def noise_aside(owner):
        noise_c(p, owner).start()

    hop(w_z, to_sections, 0)
    cond_load.wait()
    hop(cond_z, cond_aside, 0)
    noise_load.wait()

    zero_row = jnp.zeros((3 * C, cols), jnp.bfloat16)
    shifted[:, 0:cols] = zero_row
    shifted[:, (rows + 1) * cols : (rows + 2) * cols] = zero_row

    for k in range(1, chans):
        hop(w_z, to_sections, k)
        hop(cond_z, cond_aside, k)
        if k < chans - 1:
            hop(noise_z, noise_aside, k - 1)
    w_c(s, p).start()

    def forward_layer(layer):
        @pl.when(s != layer)
        def _():
            for owner in range(chans):
                w_s(0, layer, owner).wait_recv()
            w_c(layer, p).start()

    lane = lax.broadcasted_iota(jnp.int32, (C, cols), 1)
    chan_row = lax.broadcasted_iota(jnp.int32, (C, cols), 0)
    per_patch = rows // 2

    def put_row(values, row):
        base = (row + 1) * cols
        left = jnp.where(lane == 0, 0.0, pltpu.roll(values, 1, 1))
        right = jnp.where(lane == cols - 1, 0.0, pltpu.roll(values, cols - 1, 1))
        shifted[0:C, pl.ds(base, cols)] = left.astype(jnp.bfloat16)
        shifted[C : 2 * C, pl.ds(base, cols)] = values.astype(jnp.bfloat16)
        shifted[2 * C : 3 * C, pl.ds(base, cols)] = right.astype(jnp.bfloat16)

    def group_sum(values):
        total = jnp.broadcast_to(jnp.sum(values, axis=1, keepdims=True), (C, cols))
        for bit in (1, 2):
            pair = jnp.where(
                (chan_row // bit) % 2 == 0, pltpu.roll(total, C - bit, 0), pltpu.roll(total, bit, 0)
            )
            total = total + pair
        return total

    chunk_rows = 4
    chunk = chunk_rows * cols
    per_half = per_patch // chunk_rows

    def conv_and_stats(layer):
        lhs = jnp.concatenate([weights[layer, tap] for tap in range(9)], axis=1)
        sums = jnp.zeros((C, cols), jnp.float32)
        squares = jnp.zeros((C, cols), jnp.float32)
        for q in range(rows // chunk_rows):
            rhs = jnp.concatenate(
                [shifted[:, q * chunk + a * cols : q * chunk + a * cols + chunk] for a in range(3)],
                axis=0,
            )
            got = jnp.dot(lhs, rhs, preferred_element_type=jnp.float32)
            conv_f[q // per_half, :, (q % per_half) * chunk : (q % per_half + 1) * chunk] = got
            for r in range(chunk_rows):
                tile = got[:, r * cols : (r + 1) * cols]
                sums = sums + tile
                squares = squares + tile * tile
        pieces = weights[layer, 10].astype(jnp.float32)
        gain = pieces[:, 0:1] + pieces[:, 2:3] + pieces[:, 4:5]
        bias = pieces[:, 1:2] + pieces[:, 3:4] + pieces[:, 5:6]
        entries = (C // GROUPS) * cells
        mu = group_sum(sums) / entries
        var = group_sum(squares) / entries - mu * mu
        scale = 0.5 * gain / jnp.sqrt(var + 1e-05)
        return scale, 0.5 * bias - mu * scale

    def put_inputs(sample, mean, q):
        inputs = (sample.astype(jnp.float32) + mean.astype(jnp.float32)).astype(jnp.bfloat16)
        inputs = inputs.astype(jnp.float32)
        for r in range(chunk_rows):
            put_row(inputs[:, r * cols : (r + 1) * cols], q * chunk_rows + r)

    def acted_of(conv, scale, shift):
        tiles = []
        for r in range(chunk_rows):
            h = conv[:, r * cols : (r + 1) * cols] * scale + shift
            tiles.append((h + h * jnp.tanh(h)).astype(jnp.bfloat16))
        return jnp.concatenate(tiles, axis=1)

    for owner in range(chans):
        cond_c(other, owner).wait_recv()
    for row in range(rows):
        at = (row % per_patch) * cols
        put_row(cond_f[row // per_patch, :, at : at + cols].astype(jnp.float32), row)
    forward_layer(0)
    w_c(0, other).wait_recv()

    for layer in range(sections):
        last = layer == sections - 1
        scale, shift = conv_and_stats(layer)
        if layer == 0:
            hop(noise_z, noise_aside, chans - 2)
            forward_layer(1)
        if not last:
            for q in range(rows // chunk_rows):
                where = q // per_half
                span = slice((q % per_half) * chunk, (q % per_half + 1) * chunk)
                acted = acted_of(conv_f[where, :, span], scale, shift)
                out = jnp.dot(weights[layer, 9], acted, preferred_element_type=jnp.float32)
                if layer == 0:
                    mean = cond_f[where, :, span].astype(jnp.float32) + out
                    mean_f[where, :, span] = mean.astype(jnp.bfloat16)
                    continue
                before = noise_f[where, :, span].astype(jnp.float32)
                sample = (before + 0.5 * (out - before)).astype(jnp.bfloat16)
                noise_f[where, :, span] = sample
                put_inputs(sample, mean_f[where, :, span], q)
            if layer == 0:
                hop(noise_z, noise_aside, chans - 1)
                for later in range(2, sections):
                    forward_layer(later)
                for owner in range(chans):
                    noise_c(other, owner).wait_recv()
                for q in range(rows // chunk_rows):
                    where = q // per_half
                    span = slice((q % per_half) * chunk, (q % per_half + 1) * chunk)
                    put_inputs(noise_f[where, :, span], mean_f[where, :, span], q)
                sent(noise_z)
                for owner in range(chans):
                    noise_c(p, owner).wait_send()
            w_c(layer + 1, other).wait_recv()
        else:
            for q in range(per_half):
                span = slice(q * chunk, (q + 1) * chunk)
                acted = acted_of(conv_f[p, :, span], scale, shift)
                out = jnp.dot(weights[layer, 9, mine, :], acted, preferred_element_type=jnp.float32)
                before = noise_f[p, mine, span].astype(jnp.float32)
                sample = (before + 0.5 * (out - before)).astype(jnp.bfloat16).astype(jnp.float32)
                out_ref[:, span] = (sample + mean_f[p, mine, span].astype(jnp.float32)).astype(
                    jnp.bfloat16
                )

    sent(w_z)
    sent(cond_z)
    for d in range(sections - 1):
        for owner in range(chans):
            w_s(d, s, owner).wait_send()
    for layer in range(sections):
        w_c(layer, p).wait_send()
    for owner in range(chans):
        cond_c(p, owner).wait_send()


def fused_body(cond, noise, conv_weight, mix_weight, norm_gain, norm_bias):
    sections = lax.axis_size("section")
    chans = lax.axis_size("chan")
    _, part, own_rows, cols = cond.shape
    rows = 2 * own_rows
    own = own_rows * cols
    gb = jnp.where(jnp.arange(128)[None, :] % 2 == 0, norm_gain[0][:, None], norm_bias[0][:, None])
    dma = pltpu.SemaphoreType.DMA
    near, far = chans - 1, chans
    out = pl.pallas_call(
        functools.partial(whole_kernel, sections, chans, rows, cols),
        out_shape=jax.ShapeDtypeStruct((part, own), jnp.bfloat16),
        in_specs=[pl.BlockSpec(memory_space=pl.ANY)] * 4
        + [pl.BlockSpec(memory_space=pltpu.VMEM)],
        out_specs=pl.BlockSpec(memory_space=pltpu.VMEM),
        scratch_shapes=[
            pltpu.VMEM((2, C, own), jnp.bfloat16),
            pltpu.VMEM((2, C, own), jnp.bfloat16),
            pltpu.VMEM((2, C, own), jnp.bfloat16),
            pltpu.VMEM((sections, 12, C, C), jnp.bfloat16),
            pltpu.VMEM((3 * C, (rows + 2) * cols), jnp.bfloat16),
            pltpu.VMEM((2, C, own), jnp.float32),
            dma((4,)),
            dma((2, near)), dma((far,)), dma((sections - 1, far)), dma((sections, far)),
            dma((sections,)), dma((sections,)),
            dma((2, near)), dma((far,)), dma((far,)), dma((far,)),
            dma((2, near)), dma((far,)), dma((far,)), dma((far,)),
        ],
        compiler_params=pltpu.CompilerParams(
            collective_id=0, has_side_effects=True, vmem_limit_bytes=40 * 1024 * 1024
        ),
    )(
        cond.reshape(part, own), noise.reshape(part, own), conv_weight[0], mix_weight[0], gb
    )
    return out.reshape(1, part, own_rows, cols)


def solution(mesh):
    whole = mesh.shape["patch"] == 2
    return jax.shard_map(
        fused_body if whole else body,
        mesh=mesh,
        in_specs=(
            P("section", "chan", "patch", None),
            P("section", "chan", "patch", None),
            P("section", None, "chan", None),
            P("section", "chan", None),
            P("section", "chan"),
            P("section", "chan"),
        ),
        out_specs=P("section", "chan", "patch", None),
        check_vma=False,
    )
```

```python
import functools

import jax
import jax.numpy as jnp
from jax import lax
from jax.experimental import pallas as pl
from jax.experimental.pallas import tpu as pltpu
from jax.sharding import PartitionSpec as P

C = 128
GROUPS = 32


def with_halo(cells, sides, width):
    for axis, dim in sides:
        count = lax.axis_size(axis)
        ends = count - 1
        head = lax.slice_in_dim(cells, 0, width, axis=dim)
        tail = lax.slice_in_dim(cells, cells.shape[dim] - width, cells.shape[dim], axis=dim)
        cells = jnp.concatenate(
            [
                lax.ppermute(tail, axis, [(i, (i + 1) % count) for i in range(ends)]),
                cells,
                lax.ppermute(head, axis, [((i + 1) % count, i) for i in range(ends)]),
            ],
            axis=dim,
        )
    return cells


def from_root(value, axis, source):
    kept = jnp.where(lax.axis_index(axis) == source, value, 0).astype(value.dtype)
    return lax.psum(kept, axis)


def conv_taps(running, row_padded, tap_weight, num_rows, num_cols):
    padded = jnp.pad(row_padded, ((0, 0), (0, 0), (0, 0), (1, 1)))
    for tap_index in range(9):
        row_off, col_off = divmod(tap_index, 3)
        window = padded[:, :, row_off : row_off + num_rows, col_off : col_off + num_cols]
        running = running + jnp.einsum(
            "oc,bchw->bohw", tap_weight[tap_index], window, preferred_element_type=jnp.float32
        )
    return running


def group_norm(conv_total, gain_row, bias_row):
    batch_size, out_chans, num_rows, num_cols = conv_total.shape
    group_size = C // GROUPS
    grouped = conv_total.reshape(
        batch_size, out_chans // group_size, group_size, num_rows, num_cols
    )
    local_sums = jnp.sum(grouped, axis=(2, 3, 4))
    local_squares = jnp.sum(grouped * grouped, axis=(2, 3, 4))
    sums, squares = lax.psum((local_sums, local_squares), "patch")
    entries = group_size * num_rows * num_cols * lax.axis_size("patch")
    group_mean = sums / entries
    variance = squares / entries - group_mean * group_mean
    scale_now = 1.0 / jnp.sqrt(variance + 1e-05)
    normed = (grouped - group_mean[:, :, None, None, None]) * scale_now[:, :, None, None, None]
    normed = normed.reshape(batch_size, out_chans, num_rows, num_cols)
    normed = normed * gain_row[None, :, None, None] + bias_row[None, :, None, None]
    return jax.nn.silu(normed).astype(jnp.bfloat16)


def apply_block(inputs, params):
    tap_weight, mix_matrix, gain_row, bias_row = params
    batch_size = inputs.shape[0]
    num_rows = inputs.shape[2]
    num_cols = inputs.shape[3]
    out_chans = tap_weight.shape[1]
    padded = with_halo(inputs, (("patch", 2),), 1)
    empty = jnp.zeros((batch_size, out_chans, num_rows, num_cols), jnp.float32)
    weight_part = tap_weight
    conv_total = conv_taps(
        empty, lax.all_gather(padded, "chan", axis=1, tiled=True), weight_part, num_rows, num_cols
    )
    acted = group_norm(conv_total, gain_row, bias_row)
    weight_part = mix_matrix
    return jnp.einsum(
        "oc,bchw->bohw",
        weight_part,
        lax.all_gather(acted, "chan", axis=1, tiled=True),
        preferred_element_type=jnp.float32,
    )


def prepare(params):
    tap_weight = params[0][0]
    mix_matrix = params[1][0]
    gain_row = params[2][0]
    bias_row = params[3][0]
    return (tap_weight, mix_matrix, gain_row, bias_row)


def body(cond, noise, conv_weight, mix_weight, norm_gain, norm_bias):
    sections = lax.axis_size("section")
    mean_field = cond
    sample = noise
    for layer_index in range(sections):
        shared = (
            from_root(conv_weight, "section", layer_index),
            from_root(mix_weight, "section", layer_index),
            from_root(norm_gain.astype(jnp.bfloat16), "section", layer_index).astype(
                norm_gain.dtype
            ),
            from_root(norm_bias.astype(jnp.bfloat16), "section", layer_index).astype(
                norm_bias.dtype
            ),
        )
        params = prepare(shared)
        if layer_index == 0:
            first_out = apply_block(cond, params)
            mean_field = (cond.astype(jnp.float32) + first_out).astype(jnp.bfloat16)
        else:
            inputs = (sample.astype(jnp.float32) + mean_field.astype(jnp.float32)).astype(
                jnp.bfloat16
            )
            denoised = apply_block(inputs, params)
            before = sample.astype(jnp.float32)
            sample = (before + 0.5 * (denoised - before)).astype(jnp.bfloat16)
    result = (sample.astype(jnp.float32) + mean_field.astype(jnp.float32)).astype(jnp.bfloat16)
    return result


MESH = pl.DeviceIdType.MESH
AXES = ("section", "patch", "chan")


def remote(src, dst, send_sem, recv_sem, section, patch, chan):
    return pltpu.make_async_remote_copy(
        src_ref=src,
        dst_ref=dst,
        send_sem=send_sem,
        recv_sem=recv_sem,
        device_id=(section, patch, chan),
        device_id_type=MESH,
    )


def whole_kernel(
    sections, chans, rows, cols,
    cond_in, noise_in, conv_in, mix_in, gb_in, out_ref,
    cond_f, noise_f, mean_f, weights, shifted, conv_f, result, landed,
    load_sem, wz_send, wz_recv, ws_send, ws_recv, wc_send, wc_recv,
    cz_send, cz_recv, cc_send, cc_recv, nz_send, nz_recv, nc_send, nc_recv, out_send, out_recv,
):
    s = lax.axis_index("section")
    p = lax.axis_index("patch")
    z = lax.axis_index("chan")
    other = 1 - p
    taps = 12
    half = taps // 2
    part = C // chans
    cells = rows * cols
    sec_peers = [lax.rem(s + d, sections) for d in range(1, sections)]
    z_peers = [lax.rem(z + d, chans) for d in range(1, chans)]

    def band(index):
        return pl.ds(pl.multiple_of(index * part, part), part)

    mine = band(z)
    inner = (z > 0) & (z < chans - 1)
    cond_load = pltpu.make_async_copy(cond_in, cond_f.at[p, mine, :], load_sem.at[0])
    noise_load = pltpu.make_async_copy(noise_in, noise_f.at[p, mine, :], load_sem.at[1])
    mix_load = pltpu.make_async_copy(mix_in, weights.at[s, 9, mine, :], load_sem.at[2])

    def conv_load(first, count):
        return pltpu.make_async_copy(
            conv_in.at[pl.ds(first, count)],
            weights.at[s, pl.ds(first, count), mine, :],
            load_sem.at[3],
        )

    cond_load.start()

    @pl.when(p == 0)
    def _():
        conv_load(0, half).start()

    @pl.when(p != 0)
    def _():
        conv_load(half, 9 - half).start()
        mix_load.start()

    noise_load.start()

    barrier = pltpu.get_barrier_semaphore()
    for peer in sec_peers:
        pl.semaphore_signal(barrier, inc=1, device_id=(peer, p, z), device_id_type=MESH)
    for peer in z_peers:
        pl.semaphore_signal(barrier, inc=1, device_id=(s, p, peer), device_id_type=MESH)
    pl.semaphore_signal(barrier, inc=1, device_id=(s, other, z), device_id_type=MESH)
    pl.semaphore_wait(barrier, sections + chans - 1)

    @pl.when(p == 0)
    def _():
        conv_load(0, half).wait()

    @pl.when(p != 0)
    def _():
        exact = gb_in[...]
        high = exact.astype(jnp.bfloat16)
        rest = exact - high.astype(jnp.float32)
        middle = rest.astype(jnp.bfloat16)
        low = (rest - middle.astype(jnp.float32)).astype(jnp.bfloat16)
        column = lax.broadcasted_iota(jnp.int32, exact.shape, 1)
        pieces = jnp.where(
            column < 2,
            high.astype(jnp.float32),
            jnp.where(column < 4, middle.astype(jnp.float32), low.astype(jnp.float32)),
        )
        weights[s, 10, mine, :] = pieces.astype(jnp.bfloat16)
        weights[s, 11, mine, :] = jnp.zeros_like(high)
        conv_load(half, 9 - half).wait()
        mix_load.wait()

    def w_half(layer, which):
        return weights.at[layer, pl.ds(which * half, half)]

    def w_shard(layer, owner):
        return weights.at[layer, pl.ds(p * half, half), band(owner), :]

    def w_z(way, k, owner):
        block = w_shard(s, owner)
        return remote(block, block, wz_send.at[way, k], wz_recv.at[owner], s, p, z + 1 - 2 * way)

    def w_s(d, layer, owner):
        block = w_shard(layer, owner)
        return remote(block, block, ws_send.at[d, owner], ws_recv.at[layer, owner], sec_peers[d], p, z)

    def w_c(layer, which):
        return remote(w_half(layer, which), w_half(layer, which), wc_send.at[layer], wc_recv.at[layer], s, other, z)

    def f_z(field, send, recv, way, k, owner):
        block = field.at[p, band(owner), :]
        return remote(block, block, send.at[way, k], recv.at[owner], s, p, z + 1 - 2 * way)

    def f_c(field, send, recv, which, owner):
        block = field.at[which, band(owner), :]
        return remote(block, block, send.at[owner], recv.at[owner], s, other, z)

    cond_z = functools.partial(f_z, cond_f, cz_send, cz_recv)
    cond_c = functools.partial(f_c, cond_f, cc_send, cc_recv)
    noise_z = functools.partial(f_z, noise_f, nz_send, nz_recv)
    noise_c = functools.partial(f_c, noise_f, nc_send, nc_recv)

    pair = pl.ds(pl.multiple_of((z // 2) * 2 * part, 2 * part), 2 * part)
    chunk_rows = 4
    chunk = chunk_rows * cols
    per_half = rows // 2 // chunk_rows

    def give_back(q):
        span = pl.ds(q * chunk, chunk)
        away = pl.ds(pl.multiple_of((1 - z % 2) * part, part), part)
        return remote(
            result.at[away, span], landed.at[:, span], out_send.at[q], out_recv.at[q],
            s, p, (z // 2) * (chans - 1),
        )

    def to_sections(owner):
        for d in range(sections - 1):
            w_s(d, s, owner).start()

    def along(way, k):
        owner = z - k if way == 0 else z + k
        valid = z >= k if way == 0 else z + k < chans
        going = z < chans - 2 if way == 0 else z > 1
        return owner, valid & inner, valid & going

    def hop(copy, aside, k):
        if k == 0:
            for way in range(2):
                owner, _, sends = along(way, 0)

                @pl.when(sends)
                def _():
                    copy(way, 0, owner).start()

            pl.when(inner)(lambda: aside(z))
            return
        for way in range(2):
            owner, here, sends = along(way, k)

            @pl.when(here)
            def _():
                copy(way, 0, owner).wait_recv()
                if k < chans - 2:

                    @pl.when(sends)
                    def _():
                        copy(way, k, owner).start()

                aside(owner)

    def sent(copy):
        for way in range(2):
            for k in range(chans - 1):
                owner, _, sends = along(way, k)

                @pl.when(sends)
                def _():
                    copy(way, k, owner).wait_send()

    def cond_aside(owner):
        cond_c(p, owner).start()

    def noise_aside(owner):
        noise_c(p, owner).start()

    hop(w_z, to_sections, 0)
    cond_load.wait()
    hop(cond_z, cond_aside, 0)
    noise_load.wait()
    hop(noise_z, noise_aside, 0)

    @pl.when(inner)
    def _():
        zero_row = jnp.zeros((3 * C, cols), jnp.bfloat16)
        shifted[:, 0:cols] = zero_row
        shifted[:, (rows + 1) * cols : (rows + 2) * cols] = zero_row

        for k in range(1, chans - 1):
            hop(w_z, to_sections, k)
            hop(cond_z, cond_aside, k)
            if k < chans - 2:
                hop(noise_z, noise_aside, k)
        w_c(s, p).start()

        def forward_layer(layer):
            @pl.when(s != layer)
            def _():
                for owner in range(chans):
                    w_s(0, layer, owner).wait_recv()
                w_c(layer, p).start()

        lane = lax.broadcasted_iota(jnp.int32, (C, cols), 1)
        chan_row = lax.broadcasted_iota(jnp.int32, (C, cols), 0)
        per_patch = rows // 2

        def put_row(values, row):
            base = (row + 1) * cols
            left = jnp.where(lane == 0, 0.0, pltpu.roll(values, 1, 1))
            right = jnp.where(lane == cols - 1, 0.0, pltpu.roll(values, cols - 1, 1))
            shifted[0:C, pl.ds(base, cols)] = left.astype(jnp.bfloat16)
            shifted[C : 2 * C, pl.ds(base, cols)] = values.astype(jnp.bfloat16)
            shifted[2 * C : 3 * C, pl.ds(base, cols)] = right.astype(jnp.bfloat16)

        def group_sum(values):
            total = jnp.broadcast_to(jnp.sum(values, axis=1, keepdims=True), (C, cols))
            for bit in (1, 2):
                pair = jnp.where(
                    (chan_row // bit) % 2 == 0, pltpu.roll(total, C - bit, 0), pltpu.roll(total, bit, 0)
                )
                total = total + pair
            return total

        chunk_rows = 4
        chunk = chunk_rows * cols
        per_half = per_patch // chunk_rows

        def conv_and_stats(layer):
            lhs = jnp.concatenate([weights[layer, tap] for tap in range(9)], axis=1)
            sums = jnp.zeros((C, cols), jnp.float32)
            squares = jnp.zeros((C, cols), jnp.float32)
            for q in range(rows // chunk_rows):
                rhs = jnp.concatenate(
                    [shifted[:, q * chunk + a * cols : q * chunk + a * cols + chunk] for a in range(3)],
                    axis=0,
                )
                got = jnp.dot(lhs, rhs, preferred_element_type=jnp.float32)
                conv_f[q // per_half, :, (q % per_half) * chunk : (q % per_half + 1) * chunk] = got
                for r in range(chunk_rows):
                    tile = got[:, r * cols : (r + 1) * cols]
                    sums = sums + tile
                    squares = squares + tile * tile
            pieces = weights[layer, 10].astype(jnp.float32)
            gain = pieces[:, 0:1] + pieces[:, 2:3] + pieces[:, 4:5]
            bias = pieces[:, 1:2] + pieces[:, 3:4] + pieces[:, 5:6]
            entries = (C // GROUPS) * cells
            mu = group_sum(sums) / entries
            var = group_sum(squares) / entries - mu * mu
            scale = 0.5 * gain / jnp.sqrt(var + 1e-05)
            return scale, 0.5 * bias - mu * scale

        def put_inputs(sample, mean, q):
            inputs = (sample.astype(jnp.float32) + mean.astype(jnp.float32)).astype(jnp.bfloat16)
            inputs = inputs.astype(jnp.float32)
            for r in range(chunk_rows):
                put_row(inputs[:, r * cols : (r + 1) * cols], q * chunk_rows + r)

        def acted_of(conv, scale, shift):
            tiles = []
            for r in range(chunk_rows):
                h = conv[:, r * cols : (r + 1) * cols] * scale + shift
                tiles.append((h + h * jnp.tanh(h)).astype(jnp.bfloat16))
            return jnp.concatenate(tiles, axis=1)

        for owner in range(chans):
            cond_c(other, owner).wait_recv()
        for row in range(rows):
            at = (row % per_patch) * cols
            put_row(cond_f[row // per_patch, :, at : at + cols].astype(jnp.float32), row)
        forward_layer(0)
        w_c(0, other).wait_recv()

        for layer in range(sections):
            last = layer == sections - 1
            scale, shift = conv_and_stats(layer)
            if layer == 0:
                hop(noise_z, noise_aside, chans - 2)
                forward_layer(1)
            if not last:
                for q in range(rows // chunk_rows):
                    where = q // per_half
                    span = slice((q % per_half) * chunk, (q % per_half + 1) * chunk)
                    acted = acted_of(conv_f[where, :, span], scale, shift)
                    out = jnp.dot(weights[layer, 9], acted, preferred_element_type=jnp.float32)
                    if layer == 0:
                        mean = cond_f[where, :, span].astype(jnp.float32) + out
                        mean_f[where, :, span] = mean.astype(jnp.bfloat16)
                        continue
                    before = noise_f[where, :, span].astype(jnp.float32)
                    sample = (before + 0.5 * (out - before)).astype(jnp.bfloat16)
                    noise_f[where, :, span] = sample
                    put_inputs(sample, mean_f[where, :, span], q)
                if layer == 0:
                    for later in range(2, sections):
                        forward_layer(later)
                    for owner in range(chans):
                        noise_c(other, owner).wait_recv()
                    for q in range(rows // chunk_rows):
                        where = q // per_half
                        span = slice((q % per_half) * chunk, (q % per_half + 1) * chunk)
                        put_inputs(noise_f[where, :, span], mean_f[where, :, span], q)
                    sent(noise_z)
                    for owner in range(chans):
                        noise_c(p, owner).wait_send()
                w_c(layer + 1, other).wait_recv()
            else:
                for q in range(per_half):
                    span = slice(q * chunk, (q + 1) * chunk)
                    acted = acted_of(conv_f[p, :, span], scale, shift)
                    out = jnp.dot(weights[layer, 9, pair, :], acted, preferred_element_type=jnp.float32)
                    before = noise_f[p, pair, span].astype(jnp.float32)
                    sample = (before + 0.5 * (out - before)).astype(jnp.bfloat16).astype(jnp.float32)
                    result[:, span] = (sample + mean_f[p, pair, span].astype(jnp.float32)).astype(
                        jnp.bfloat16
                    )
                    give_back(q).start()
                    out_ref[:, span] = result[pl.ds(pl.multiple_of((z % 2) * part, part), part), span]
        for d in range(sections - 1):
            for owner in range(chans):
                w_s(d, s, owner).wait_send()
        for layer in range(sections):
            w_c(layer, p).wait_send()
        for owner in range(chans):
            cond_c(p, owner).wait_send()
        for q in range(per_half):
            give_back(q).wait_send()

    @pl.when(jnp.logical_not(inner))
    def _():
        sent(noise_z)
        for q in range(per_half):
            give_back(q).wait_recv()
        out_ref[...] = landed[...]

    sent(w_z)
    sent(cond_z)


def fused_body(cond, noise, conv_weight, mix_weight, norm_gain, norm_bias):
    sections = lax.axis_size("section")
    chans = lax.axis_size("chan")
    _, part, own_rows, cols = cond.shape
    rows = 2 * own_rows
    own = own_rows * cols
    gb = jnp.where(jnp.arange(128)[None, :] % 2 == 0, norm_gain[0][:, None], norm_bias[0][:, None])
    dma = pltpu.SemaphoreType.DMA
    near, far = chans - 1, chans
    out = pl.pallas_call(
        functools.partial(whole_kernel, sections, chans, rows, cols),
        out_shape=jax.ShapeDtypeStruct((part, own), jnp.bfloat16),
        in_specs=[pl.BlockSpec(memory_space=pl.ANY)] * 4
        + [pl.BlockSpec(memory_space=pltpu.VMEM)],
        out_specs=pl.BlockSpec(memory_space=pltpu.VMEM),
        scratch_shapes=[
            pltpu.VMEM((2, C, own), jnp.bfloat16),
            pltpu.VMEM((2, C, own), jnp.bfloat16),
            pltpu.VMEM((2, C, own), jnp.bfloat16),
            pltpu.VMEM((sections, 12, C, C), jnp.bfloat16),
            pltpu.VMEM((3 * C, (rows + 2) * cols), jnp.bfloat16),
            pltpu.VMEM((2, C, own), jnp.float32),
            pltpu.VMEM((2 * part, own), jnp.bfloat16),
            pltpu.VMEM((part, own), jnp.bfloat16),
            dma((4,)),
            dma((2, near)), dma((far,)), dma((sections - 1, far)), dma((sections, far)),
            dma((sections,)), dma((sections,)),
            dma((2, near)), dma((far,)), dma((far,)), dma((far,)),
            dma((2, near)), dma((far,)), dma((far,)), dma((far,)),
            dma((2,)), dma((2,)),
        ],
        compiler_params=pltpu.CompilerParams(
            collective_id=0, has_side_effects=True, vmem_limit_bytes=40 * 1024 * 1024
        ),
    )(
        cond.reshape(part, own), noise.reshape(part, own), conv_weight[0], mix_weight[0], gb
    )
    return out.reshape(1, part, own_rows, cols)


def solution(mesh):
    whole = mesh.shape["patch"] == 2 and mesh.shape["chan"] == 4
    return jax.shard_map(
        fused_body if whole else body,
        mesh=mesh,
        in_specs=(
            P("section", "chan", "patch", None),
            P("section", "chan", "patch", None),
            P("section", None, "chan", None),
            P("section", "chan", None),
            P("section", "chan"),
            P("section", "chan"),
        ),
        out_specs=P("section", "chan", "patch", None),
        check_vma=False,
    )
```

```python
import functools

import jax
import jax.numpy as jnp
from jax import lax
from jax.experimental import pallas as pl
from jax.experimental.pallas import tpu as pltpu
from jax.sharding import PartitionSpec as P

C = 128
GROUPS = 32


def with_halo(cells, sides, width):
    for axis, dim in sides:
        count = lax.axis_size(axis)
        ends = count - 1
        head = lax.slice_in_dim(cells, 0, width, axis=dim)
        tail = lax.slice_in_dim(cells, cells.shape[dim] - width, cells.shape[dim], axis=dim)
        cells = jnp.concatenate(
            [
                lax.ppermute(tail, axis, [(i, (i + 1) % count) for i in range(ends)]),
                cells,
                lax.ppermute(head, axis, [((i + 1) % count, i) for i in range(ends)]),
            ],
            axis=dim,
        )
    return cells


def from_root(value, axis, source):
    kept = jnp.where(lax.axis_index(axis) == source, value, 0).astype(value.dtype)
    return lax.psum(kept, axis)


def conv_taps(running, row_padded, tap_weight, num_rows, num_cols):
    padded = jnp.pad(row_padded, ((0, 0), (0, 0), (0, 0), (1, 1)))
    for tap_index in range(9):
        row_off, col_off = divmod(tap_index, 3)
        window = padded[:, :, row_off : row_off + num_rows, col_off : col_off + num_cols]
        running = running + jnp.einsum(
            "oc,bchw->bohw", tap_weight[tap_index], window, preferred_element_type=jnp.float32
        )
    return running


def group_norm(conv_total, gain_row, bias_row):
    batch_size, out_chans, num_rows, num_cols = conv_total.shape
    group_size = C // GROUPS
    grouped = conv_total.reshape(
        batch_size, out_chans // group_size, group_size, num_rows, num_cols
    )
    local_sums = jnp.sum(grouped, axis=(2, 3, 4))
    local_squares = jnp.sum(grouped * grouped, axis=(2, 3, 4))
    sums, squares = lax.psum((local_sums, local_squares), "patch")
    entries = group_size * num_rows * num_cols * lax.axis_size("patch")
    group_mean = sums / entries
    variance = squares / entries - group_mean * group_mean
    scale_now = 1.0 / jnp.sqrt(variance + 1e-05)
    normed = (grouped - group_mean[:, :, None, None, None]) * scale_now[:, :, None, None, None]
    normed = normed.reshape(batch_size, out_chans, num_rows, num_cols)
    normed = normed * gain_row[None, :, None, None] + bias_row[None, :, None, None]
    return jax.nn.silu(normed).astype(jnp.bfloat16)


def apply_block(inputs, params):
    tap_weight, mix_matrix, gain_row, bias_row = params
    batch_size = inputs.shape[0]
    num_rows = inputs.shape[2]
    num_cols = inputs.shape[3]
    out_chans = tap_weight.shape[1]
    padded = with_halo(inputs, (("patch", 2),), 1)
    empty = jnp.zeros((batch_size, out_chans, num_rows, num_cols), jnp.float32)
    weight_part = tap_weight
    conv_total = conv_taps(
        empty, lax.all_gather(padded, "chan", axis=1, tiled=True), weight_part, num_rows, num_cols
    )
    acted = group_norm(conv_total, gain_row, bias_row)
    weight_part = mix_matrix
    return jnp.einsum(
        "oc,bchw->bohw",
        weight_part,
        lax.all_gather(acted, "chan", axis=1, tiled=True),
        preferred_element_type=jnp.float32,
    )


def prepare(params):
    tap_weight = params[0][0]
    mix_matrix = params[1][0]
    gain_row = params[2][0]
    bias_row = params[3][0]
    return (tap_weight, mix_matrix, gain_row, bias_row)


def body(cond, noise, conv_weight, mix_weight, norm_gain, norm_bias):
    sections = lax.axis_size("section")
    mean_field = cond
    sample = noise
    for layer_index in range(sections):
        shared = (
            from_root(conv_weight, "section", layer_index),
            from_root(mix_weight, "section", layer_index),
            from_root(norm_gain.astype(jnp.bfloat16), "section", layer_index).astype(
                norm_gain.dtype
            ),
            from_root(norm_bias.astype(jnp.bfloat16), "section", layer_index).astype(
                norm_bias.dtype
            ),
        )
        params = prepare(shared)
        if layer_index == 0:
            first_out = apply_block(cond, params)
            mean_field = (cond.astype(jnp.float32) + first_out).astype(jnp.bfloat16)
        else:
            inputs = (sample.astype(jnp.float32) + mean_field.astype(jnp.float32)).astype(
                jnp.bfloat16
            )
            denoised = apply_block(inputs, params)
            before = sample.astype(jnp.float32)
            sample = (before + 0.5 * (denoised - before)).astype(jnp.bfloat16)
    result = (sample.astype(jnp.float32) + mean_field.astype(jnp.float32)).astype(jnp.bfloat16)
    return result


MESH = pl.DeviceIdType.MESH
AXES = ("section", "patch", "chan")


def remote(src, dst, send_sem, recv_sem, section, patch, chan):
    return pltpu.make_async_remote_copy(
        src_ref=src,
        dst_ref=dst,
        send_sem=send_sem,
        recv_sem=recv_sem,
        device_id=(section, patch, chan),
        device_id_type=MESH,
    )


def whole_kernel(
    sections, chans, rows, cols,
    cond_in, noise_in, conv_in, mix_in, gb_in, out_ref,
    cond_f, noise_f, mean_f, weights, shifted, conv_f, result, landed,
    load_sem, wz_send, wz_recv, ws_send, ws_recv, wc_send, wc_recv,
    cz_send, cz_recv, cc_send, cc_recv, nz_send, nz_recv, nc_send, nc_recv, out_send, out_recv,
):
    s = lax.axis_index("section")
    p = lax.axis_index("patch")
    z = lax.axis_index("chan")
    other = 1 - p
    taps = 12
    half = taps // 2
    part = C // chans
    cells = rows * cols
    sec_peers = [lax.rem(s + d, sections) for d in range(1, sections)]

    def band(index):
        return pl.ds(pl.multiple_of(index * part, part), part)

    mine = band(z)
    inner = (z > 0) & (z < chans - 1)
    cond_load = pltpu.make_async_copy(cond_in, cond_f.at[p, mine, :], load_sem.at[0])
    noise_load = pltpu.make_async_copy(noise_in, noise_f.at[p, mine, :], load_sem.at[1])
    mix_load = pltpu.make_async_copy(mix_in, weights.at[s, 9, mine, :], load_sem.at[2])

    def conv_load(first, count):
        return pltpu.make_async_copy(
            conv_in.at[pl.ds(first, count)],
            weights.at[s, pl.ds(first, count), mine, :],
            load_sem.at[3],
        )

    cond_load.start()

    @pl.when(p == 0)
    def _():
        conv_load(0, half).start()

    @pl.when(p != 0)
    def _():
        conv_load(half, 9 - half).start()
        mix_load.start()

    noise_load.start()

    barrier = pltpu.get_barrier_semaphore()
    for step in (-1, 1):

        @pl.when((z + step >= 0) & (z + step < chans))
        def _():
            pl.semaphore_signal(barrier, inc=1, device_id=(s, p, z + step), device_id_type=MESH)

    @pl.when(inner)
    def _():
        for peer in sec_peers:
            pl.semaphore_signal(barrier, inc=1, device_id=(peer, p, z), device_id_type=MESH)
        pl.semaphore_signal(barrier, inc=1, device_id=(s, other, z), device_id_type=MESH)

    pl.semaphore_wait(barrier, jnp.where(inner, sections + 2, 1))

    @pl.when(p == 0)
    def _():
        conv_load(0, half).wait()

    @pl.when(p != 0)
    def _():
        exact = gb_in[...]
        high = exact.astype(jnp.bfloat16)
        rest = exact - high.astype(jnp.float32)
        middle = rest.astype(jnp.bfloat16)
        low = (rest - middle.astype(jnp.float32)).astype(jnp.bfloat16)
        column = lax.broadcasted_iota(jnp.int32, exact.shape, 1)
        pieces = jnp.where(
            column < 2,
            high.astype(jnp.float32),
            jnp.where(column < 4, middle.astype(jnp.float32), low.astype(jnp.float32)),
        )
        weights[s, 10, mine, :] = pieces.astype(jnp.bfloat16)
        weights[s, 11, mine, :] = jnp.zeros_like(high)
        conv_load(half, 9 - half).wait()
        mix_load.wait()

    def w_half(layer, which):
        return weights.at[layer, pl.ds(which * half, half)]

    def w_shard(layer, owner):
        return weights.at[layer, pl.ds(p * half, half), band(owner), :]

    def w_z(way, k, owner):
        block = w_shard(s, owner)
        return remote(block, block, wz_send.at[way, k], wz_recv.at[owner], s, p, z + 1 - 2 * way)

    def w_s(d, layer, owner):
        block = w_shard(layer, owner)
        return remote(block, block, ws_send.at[d, owner], ws_recv.at[layer, owner], sec_peers[d], p, z)

    def w_c(layer, which):
        return remote(w_half(layer, which), w_half(layer, which), wc_send.at[layer], wc_recv.at[layer], s, other, z)

    def f_z(field, send, recv, way, k, owner):
        block = field.at[p, band(owner), :]
        return remote(block, block, send.at[way, k], recv.at[owner], s, p, z + 1 - 2 * way)

    def f_c(field, send, recv, which, owner):
        block = field.at[which, band(owner), :]
        return remote(block, block, send.at[owner], recv.at[owner], s, other, z)

    cond_z = functools.partial(f_z, cond_f, cz_send, cz_recv)
    cond_c = functools.partial(f_c, cond_f, cc_send, cc_recv)
    noise_z = functools.partial(f_z, noise_f, nz_send, nz_recv)
    noise_c = functools.partial(f_c, noise_f, nc_send, nc_recv)

    pair = pl.ds(pl.multiple_of((z // 2) * 2 * part, 2 * part), 2 * part)
    chunk_rows = 4
    chunk = chunk_rows * cols
    per_half = rows // 2 // chunk_rows

    def give_back(q):
        span = pl.ds(q * chunk, chunk)
        away = pl.ds(pl.multiple_of((1 - z % 2) * part, part), part)
        return remote(
            result.at[away, span], landed.at[:, span], out_send.at[q], out_recv.at[q],
            s, p, (z // 2) * (chans - 1),
        )

    def to_sections(owner):
        for d in range(sections - 1):
            w_s(d, s, owner).start()

    def along(way, k):
        owner = z - k if way == 0 else z + k
        valid = z >= k if way == 0 else z + k < chans
        going = z < chans - 2 if way == 0 else z > 1
        return owner, valid & inner, valid & going

    def hop(copy, aside, k):
        if k == 0:
            for way in range(2):
                owner, _, sends = along(way, 0)

                @pl.when(sends)
                def _():
                    copy(way, 0, owner).start()

            pl.when(inner)(lambda: aside(z))
            return
        for way in range(2):
            owner, here, sends = along(way, k)

            @pl.when(here)
            def _():
                copy(way, 0, owner).wait_recv()
                if k < chans - 2:

                    @pl.when(sends)
                    def _():
                        copy(way, k, owner).start()

                aside(owner)

    def sent(copy):
        for way in range(2):
            for k in range(chans - 1):
                owner, _, sends = along(way, k)

                @pl.when(sends)
                def _():
                    copy(way, k, owner).wait_send()

    def cond_aside(owner):
        cond_c(p, owner).start()

    def noise_aside(owner):
        noise_c(p, owner).start()

    hop(w_z, to_sections, 0)
    cond_load.wait()
    hop(cond_z, cond_aside, 0)
    noise_load.wait()
    hop(noise_z, noise_aside, 0)

    @pl.when(inner)
    def _():
        zero_row = jnp.zeros((3 * C, cols), jnp.bfloat16)
        shifted[:, 0:cols] = zero_row
        shifted[:, (rows + 1) * cols : (rows + 2) * cols] = zero_row

        for k in range(1, chans - 1):
            hop(w_z, to_sections, k)
            hop(cond_z, cond_aside, k)
            if k < chans - 2:
                hop(noise_z, noise_aside, k)
        w_c(s, p).start()

        def forward_layer(layer):
            @pl.when(s != layer)
            def _():
                for owner in range(chans):
                    w_s(0, layer, owner).wait_recv()
                w_c(layer, p).start()

        lane = lax.broadcasted_iota(jnp.int32, (C, cols), 1)
        chan_row = lax.broadcasted_iota(jnp.int32, (C, cols), 0)
        per_patch = rows // 2

        def put_row(values, row):
            base = (row + 1) * cols
            left = jnp.where(lane == 0, 0.0, pltpu.roll(values, 1, 1))
            right = jnp.where(lane == cols - 1, 0.0, pltpu.roll(values, cols - 1, 1))
            shifted[0:C, pl.ds(base, cols)] = left.astype(jnp.bfloat16)
            shifted[C : 2 * C, pl.ds(base, cols)] = values.astype(jnp.bfloat16)
            shifted[2 * C : 3 * C, pl.ds(base, cols)] = right.astype(jnp.bfloat16)

        def group_sum(values):
            total = jnp.broadcast_to(jnp.sum(values, axis=1, keepdims=True), (C, cols))
            for bit in (1, 2):
                pair = jnp.where(
                    (chan_row // bit) % 2 == 0, pltpu.roll(total, C - bit, 0), pltpu.roll(total, bit, 0)
                )
                total = total + pair
            return total

        chunk_rows = 4
        chunk = chunk_rows * cols
        per_half = per_patch // chunk_rows

        def conv_and_stats(layer):
            lhs = jnp.concatenate([weights[layer, tap] for tap in range(9)], axis=1)
            sums = jnp.zeros((C, cols), jnp.float32)
            squares = jnp.zeros((C, cols), jnp.float32)
            for q in range(rows // chunk_rows):
                rhs = jnp.concatenate(
                    [shifted[:, q * chunk + a * cols : q * chunk + a * cols + chunk] for a in range(3)],
                    axis=0,
                )
                got = jnp.dot(lhs, rhs, preferred_element_type=jnp.float32)
                conv_f[q // per_half, :, (q % per_half) * chunk : (q % per_half + 1) * chunk] = got
                for r in range(chunk_rows):
                    tile = got[:, r * cols : (r + 1) * cols]
                    sums = sums + tile
                    squares = squares + tile * tile
            pieces = weights[layer, 10].astype(jnp.float32)
            gain = pieces[:, 0:1] + pieces[:, 2:3] + pieces[:, 4:5]
            bias = pieces[:, 1:2] + pieces[:, 3:4] + pieces[:, 5:6]
            entries = (C // GROUPS) * cells
            mu = group_sum(sums) / entries
            var = group_sum(squares) / entries - mu * mu
            scale = 0.5 * gain / jnp.sqrt(var + 1e-05)
            return scale, 0.5 * bias - mu * scale

        def put_inputs(sample, mean, q):
            inputs = (sample.astype(jnp.float32) + mean.astype(jnp.float32)).astype(jnp.bfloat16)
            inputs = inputs.astype(jnp.float32)
            for r in range(chunk_rows):
                put_row(inputs[:, r * cols : (r + 1) * cols], q * chunk_rows + r)

        def acted_of(conv, scale, shift):
            tiles = []
            for r in range(chunk_rows):
                h = conv[:, r * cols : (r + 1) * cols] * scale + shift
                tiles.append((h + h * jnp.tanh(h)).astype(jnp.bfloat16))
            return jnp.concatenate(tiles, axis=1)

        for owner in range(chans):
            cond_c(other, owner).wait_recv()
        for row in range(rows):
            at = (row % per_patch) * cols
            put_row(cond_f[row // per_patch, :, at : at + cols].astype(jnp.float32), row)
        forward_layer(0)
        w_c(0, other).wait_recv()

        for layer in range(sections):
            last = layer == sections - 1
            scale, shift = conv_and_stats(layer)
            if layer == 0:
                hop(noise_z, noise_aside, chans - 2)
                forward_layer(1)
            if not last:
                for q in range(rows // chunk_rows):
                    where = q // per_half
                    span = slice((q % per_half) * chunk, (q % per_half + 1) * chunk)
                    acted = acted_of(conv_f[where, :, span], scale, shift)
                    out = jnp.dot(weights[layer, 9], acted, preferred_element_type=jnp.float32)
                    if layer == 0:
                        mean = cond_f[where, :, span].astype(jnp.float32) + out
                        mean_f[where, :, span] = mean.astype(jnp.bfloat16)
                        continue
                    before = noise_f[where, :, span].astype(jnp.float32)
                    sample = (before + 0.5 * (out - before)).astype(jnp.bfloat16)
                    noise_f[where, :, span] = sample
                    put_inputs(sample, mean_f[where, :, span], q)
                if layer == 0:
                    for later in range(2, sections):
                        forward_layer(later)
                    for owner in range(chans):
                        noise_c(other, owner).wait_recv()
                    for q in range(rows // chunk_rows):
                        where = q // per_half
                        span = slice((q % per_half) * chunk, (q % per_half + 1) * chunk)
                        put_inputs(noise_f[where, :, span], mean_f[where, :, span], q)
                    sent(noise_z)
                    for owner in range(chans):
                        noise_c(p, owner).wait_send()
                w_c(layer + 1, other).wait_recv()
            else:
                for q in range(per_half):
                    span = slice(q * chunk, (q + 1) * chunk)
                    acted = acted_of(conv_f[p, :, span], scale, shift)
                    out = jnp.dot(weights[layer, 9, pair, :], acted, preferred_element_type=jnp.float32)
                    before = noise_f[p, pair, span].astype(jnp.float32)
                    sample = (before + 0.5 * (out - before)).astype(jnp.bfloat16).astype(jnp.float32)
                    result[:, span] = (sample + mean_f[p, pair, span].astype(jnp.float32)).astype(
                        jnp.bfloat16
                    )
                    give_back(q).start()
                    out_ref[:, span] = result[pl.ds(pl.multiple_of((z % 2) * part, part), part), span]
        for d in range(sections - 1):
            for owner in range(chans):
                w_s(d, s, owner).wait_send()
        for layer in range(sections):
            w_c(layer, p).wait_send()
        for owner in range(chans):
            cond_c(p, owner).wait_send()
        for q in range(per_half):
            give_back(q).wait_send()

    @pl.when(jnp.logical_not(inner))
    def _():
        sent(noise_z)
        for q in range(per_half):
            give_back(q).wait_recv()
        out_ref[...] = landed[...]

    sent(w_z)
    sent(cond_z)


def fused_body(cond, noise, conv_weight, mix_weight, norm_gain, norm_bias):
    sections = lax.axis_size("section")
    chans = lax.axis_size("chan")
    _, part, own_rows, cols = cond.shape
    rows = 2 * own_rows
    own = own_rows * cols
    gb = jnp.where(jnp.arange(128)[None, :] % 2 == 0, norm_gain[0][:, None], norm_bias[0][:, None])
    dma = pltpu.SemaphoreType.DMA
    near, far = chans - 1, chans
    out = pl.pallas_call(
        functools.partial(whole_kernel, sections, chans, rows, cols),
        out_shape=jax.ShapeDtypeStruct((part, own), jnp.bfloat16),
        in_specs=[pl.BlockSpec(memory_space=pl.ANY)] * 4
        + [pl.BlockSpec(memory_space=pltpu.VMEM)],
        out_specs=pl.BlockSpec(memory_space=pltpu.VMEM),
        scratch_shapes=[
            pltpu.VMEM((2, C, own), jnp.bfloat16),
            pltpu.VMEM((2, C, own), jnp.bfloat16),
            pltpu.VMEM((2, C, own), jnp.bfloat16),
            pltpu.VMEM((sections, 12, C, C), jnp.bfloat16),
            pltpu.VMEM((3 * C, (rows + 2) * cols), jnp.bfloat16),
            pltpu.VMEM((2, C, own), jnp.float32),
            pltpu.VMEM((2 * part, own), jnp.bfloat16),
            pltpu.VMEM((part, own), jnp.bfloat16),
            dma((4,)),
            dma((2, near)), dma((far,)), dma((sections - 1, far)), dma((sections, far)),
            dma((sections,)), dma((sections,)),
            dma((2, near)), dma((far,)), dma((far,)), dma((far,)),
            dma((2, near)), dma((far,)), dma((far,)), dma((far,)),
            dma((2,)), dma((2,)),
        ],
        compiler_params=pltpu.CompilerParams(
            collective_id=0, has_side_effects=True, vmem_limit_bytes=40 * 1024 * 1024
        ),
    )(
        cond.reshape(part, own), noise.reshape(part, own), conv_weight[0], mix_weight[0], gb
    )
    return out.reshape(1, part, own_rows, cols)


def solution(mesh):
    whole = mesh.shape["patch"] == 2 and mesh.shape["chan"] == 4
    return jax.shard_map(
        fused_body if whole else body,
        mesh=mesh,
        in_specs=(
            P("section", "chan", "patch", None),
            P("section", "chan", "patch", None),
            P("section", None, "chan", None),
            P("section", "chan", None),
            P("section", "chan"),
            P("section", "chan"),
        ),
        out_specs=P("section", "chan", "patch", None),
        check_vma=False,
    )
```
